32 devices in a mesh: outer: 2 (over core), row: 16 (over z, y, x).
Axes of the slice: x: 2, y: 2, z: 4, core: 2. Of those that a mesh axis runs over, the one named last changes fastest.
Arguments:
- grad_gate: bfloat16 [2, 8192, 14336], P('outer', 'row'), may hold values from -6 to 6
- grad_up: bfloat16 [2, 8192, 14336], P('outer', 'row'), may hold values from -6 to 6
- basis_gate: bfloat16 [32, 14336], P(None, 'row'), may hold values from -0.046875 to 0.046875
- basis_up: bfloat16 [32, 14336], P(None, 'row'), may hold values from -0.046875 to 0.046875
Outputs:
- next_gate: float32 [32, 14336], P(None, 'row')
- next_up: float32 [32, 14336], P(None, 'row')
- factor_gate: float32 [8192, 32], P('row')
- factor_up: float32 [8192, 32], P('row')
- resid_gate: bfloat16 [2, 8192, 14336], P('outer', 'row')
- resid_up: bfloat16 [2, 8192, 14336], P('outer', 'row')
The draws below stay inside these ranges and needn't reach their ends.
All inputs are finite; a program needn't handle non-finite values.
Results may differ from the reference program's by a relative error of at most 0.005.
Values may be sent and summed in bfloat16 or wider, within the bound.
A program may use at most 128 MiB of HBM per device.

```python
import jax
import jax.numpy as jnp
from jax import lax

D = 8192
N = 14336
R = 32
PODS = 2


def strengthened(entries, rng, source, target, parts, factor):
    def block_of(position):
        return (jnp.arange(entries.shape[position]) // (entries.shape[position] // parts)).reshape((-1,) + (1,) * (entries.ndim - 1 - position))

    one_side = jax.random.permutation(rng, parts)[block_of(target)]
    second = (block_of(target) + parts // 2) % parts
    return jnp.where((block_of(source) == one_side) | (block_of(source) == second), factor * entries, entries)


def level_of(own_key, dims, pieces, smallest, largest):
    loudness = 1.0
    for dim, shards_of in pieces:
        heights = jax.random.uniform(jax.random.fold_in(jax.random.fold_in(own_key, 6), dim), (shards_of,), jnp.float32, smallest / len(pieces), largest / len(pieces))
        loudness = loudness * jnp.repeat(jnp.exp(heights), dims[dim] // shards_of).reshape((-1,) + (1,) * (len(dims) - 1 - dim))
    return loudness


def scatter_about(rng, extent, spread, most, shards=(), dtype=jnp.bfloat16):
    entries = jax.random.normal(rng, extent, jnp.float32) * spread
    if len(shards) > 0:
        entries = level_of(rng, extent, shards, -0.22, 0.18) * entries
    return jnp.clip(entries, min=-most, max=most).astype(dtype)


def noise_with(rng, dims, width, reach, cuts, heavy, dtype=jnp.bfloat16):
    drawn = width * jax.random.normal(rng, dims, jnp.float32)
    if cuts:
        drawn = drawn * level_of(rng, dims, cuts, -0.22, 0.18)
    return jnp.clip(strengthened(drawn, jax.random.fold_in(rng, 3), *heavy), -reach, reach).astype(dtype)


def setup_inputs(seed: int = 0) -> dict:
    arg_keys = jax.random.split(jax.random.key(seed), 5)
    return {
        "grad_gate": noise_with(arg_keys[0], (PODS, D, N), 1.0, 6.0, ((0, 2), (1, 16)), (1, 2, 16, 2.0)),
        "grad_up": noise_with(arg_keys[1], (PODS, D, N), 1.0, 6.0, ((0, 2), (1, 16)), (1, 2, 16, 2.0)),
        "basis_gate": scatter_about(arg_keys[2], (R, N), N ** -0.5, 0.046875, ((1, 16),)),
        "basis_up": scatter_about(arg_keys[3], (R, N), N ** -0.5, 0.046875, ((1, 16),)),
    }


def forward_solve(lower_matrix, right_hand):
    return jax.scipy.linalg.solve_triangular(lower_matrix, right_hand, lower=True)

def compress(gradient, previous):
    pod_count = gradient.shape[0]
    accumulated = jnp.zeros((gradient.shape[1], previous.shape[0]), jnp.float32)
    for pod_index in range(pod_count):
        accumulated = accumulated + jnp.dot(gradient[pod_index].astype(jnp.float32), previous.T.astype(jnp.float32), preferred_element_type=jnp.float32)
    rounded = (accumulated / pod_count).astype(jnp.bfloat16)
    gram_matrix = jnp.dot(rounded.T.astype(jnp.float32), rounded.astype(jnp.float32), preferred_element_type=jnp.float32)
    cholesky_factor = jnp.linalg.cholesky(gram_matrix)
    products = jnp.zeros((previous.shape[0], gradient.shape[2]), jnp.float32)
    for pod_index in range(pod_count):
        products = products + jnp.dot(rounded.T.astype(jnp.float32), gradient[pod_index].astype(jnp.float32), preferred_element_type=jnp.float32)
    products = products / pod_count
    next_basis = forward_solve(cholesky_factor, products)
    factor = forward_solve(cholesky_factor, rounded.astype(jnp.float32).T).T
    approximation = jnp.dot(factor, next_basis, precision=lax.Precision.HIGHEST)
    residuals = []
    for pod_index in range(pod_count):
        residuals.append((gradient[pod_index].astype(jnp.float32) - approximation).astype(jnp.bfloat16))
    return (next_basis, factor, jnp.stack(residuals))

def reference(grad_gate, grad_up, basis_gate, basis_up):
    next_gate, factor_gate, resid_gate = compress(grad_gate, basis_gate)
    next_up, factor_up, resid_up = compress(grad_up, basis_up)
    return (next_gate, next_up, factor_gate, factor_up, resid_gate, resid_up)
```

```python
import functools

import jax
import jax.numpy as jnp
from jax import lax
from jax.experimental import pallas as pl
from jax.experimental.pallas import tpu as pltpu
from jax.sharding import PartitionSpec as P

MESH = pl.DeviceIdType.MESH
HIGHEST = lax.Precision.HIGHEST


def forward_solve(lower_matrix, right_hand):
    return jax.scipy.linalg.solve_triangular(lower_matrix, right_hand, lower=True)


def contract_cols(left, right):
    return lax.dot_general(
        left, right, (((1,), (1,)), ((), ())), preferred_element_type=jnp.float32
    )


def contract_rows(left, right):
    return lax.dot_general(
        left, right, (((0,), (0,)), ((), ())), preferred_element_type=jnp.float32
    )


def local(grad_gate, grad_up, basis_gate, basis_up):
    pod_count = lax.axis_size("outer")
    gate_rows = grad_gate[0]
    up_rows = grad_up[0]
    full_cols = gate_rows.shape[1]
    summed = lax.psum(
        (
            contract_cols(gate_rows, lax.all_gather(basis_gate, "row", axis=1, tiled=True)),
            contract_cols(up_rows, lax.all_gather(basis_up, "row", axis=1, tiled=True)),
        ),
        "outer",
    )
    round_gate = (summed[0] / pod_count).astype(jnp.bfloat16)
    round_up = (summed[1] / pod_count).astype(jnp.bfloat16)
    gram_pair = lax.psum(
        (contract_rows(round_gate, round_gate), contract_rows(round_up, round_up)), "row"
    )
    lower_gate = jnp.linalg.cholesky(gram_pair[0])
    lower_up = jnp.linalg.cholesky(gram_pair[1])
    products = (contract_rows(round_gate, gate_rows), contract_rows(round_up, up_rows))
    shard_cols = full_cols // lax.axis_size("row")
    shard_start = lax.axis_index("row") * shard_cols
    totals = lax.psum((products[0], products[1]), ("outer", "row"))
    full_gate = forward_solve(lower_gate, totals[0] / pod_count)
    full_up = forward_solve(lower_up, totals[1] / pod_count)
    next_gate = lax.dynamic_slice_in_dim(full_gate, shard_start, shard_cols, 1)
    next_up = lax.dynamic_slice_in_dim(full_up, shard_start, shard_cols, 1)
    factor_gate = forward_solve(lower_gate, round_gate.astype(jnp.float32).T).T
    factor_up = forward_solve(lower_up, round_up.astype(jnp.float32).T).T
    resid_gate = (
        gate_rows - jnp.dot(factor_gate, full_gate, precision=lax.Precision.HIGHEST)
    ).astype(jnp.bfloat16)
    resid_up = (up_rows - jnp.dot(factor_up, full_up, precision=lax.Precision.HIGHEST)).astype(
        jnp.bfloat16
    )
    return (next_gate, next_up, factor_gate, factor_up, resid_gate[None], resid_up[None])


def gather_kernel(
    n, pods, g0_ref, g1_ref, b0_ref, b1_ref,
    s0_ref, s1_ref, prt_ref, linv_ref, own_ref,
    grads, basis, sfull, acc, csend, crecv, rsend, rrecv, pacc, ptsend, ptrecv,
    gsend, grecv, own, send_sems, recv_sems, g_sems, out_sems,
):
    m = n.bit_length() - 1
    Q = n // 4
    me = lax.axis_index("row")
    core = lax.axis_index("outer")
    rank = prt_ref.shape[1]
    half = rank // 2
    cols = b0_ref.shape[1]
    grad_refs = (g0_ref, g1_ref)
    basis_refs = (b0_ref, b1_ref)
    out_refs = (s0_ref, s1_ref)

    delta = [(1 - 2 * ((me // 2**b) % 2)) * 2**b for b in range(m)]
    slot_delta = [delta[m - 1 - i] for i in range(m - 2)] + [delta[0], delta[1]]

    def block_of(q):
        place = me
        for i in range(m):
            place = place + ((q // 2**i) % 2) * slot_delta[i]
        return place

    near = {"row": me + (1 - core) * delta[0] + core * delta[1]}
    far = {"row": me + (1 - core) * delta[1] + core * delta[0]}
    partner = [{"row": me + delta[m - 1 - i]} for i in range(m - 2)]
    twin = {"outer": 1 - core}

    used = [0]
    sent = []

    def push(src, dst, target):
        i = used[0]
        used[0] += 1
        copy = pltpu.make_async_remote_copy(
            src_ref=src, dst_ref=dst, send_sem=send_sems.at[i], recv_sem=recv_sems.at[i],
            device_id=target, device_id_type=MESH,
        )
        copy.start()
        sent.append(copy)
        return copy

    def load(mat, q):
        start = pl.multiple_of(block_of(q) * cols, 128)
        return pltpu.make_async_copy(
            grad_refs[mat].at[0, :, pl.ds(start, cols)], grads.at[mat, q],
            g_sems.at[mat * n + q],
        )

    def load_all(mat):
        @pl.loop(0, n)
        def _(q):
            load(mat, q).start()

    barrier = pltpu.get_barrier_semaphore()
    greeted = partner + [{"row": me + delta[0]}, {"row": me + delta[1]}, twin]
    for target in greeted:
        pl.semaphore_signal(barrier, inc=1, device_id=target, device_id_type=MESH)
    load_all(0)
    load_all(1)
    for mat in range(2):
        basis[mat, 0] = basis_refs[mat][...].reshape(2, half, cols)
        pacc[mat] = jnp.zeros(pacc.shape[1:], jnp.float32)
    pl.semaphore_wait(barrier, len(greeted))

    class Gather:
        def __init__(self, ref):
            self.ref = ref
            self.moves = {}
            self.swaps = {}

        def go(self, name, src, dst, size, target):
            self.moves[name] = (
                push(
                    self.ref.at[pl.ds(src, size), core], self.ref.at[pl.ds(dst, size), core], target
                ),
                dst,
                size,
            )

        def start(self, i):
            if i < m - 2:
                self.go(i, 0, 2**i, 2**i, partner[i])
            elif i == m - 2:
                self.go("near", 0, (1 + core) * Q, Q, near)
                self.go("far", 0, (2 - core) * Q, Q, far)
            else:
                self.go("last", (1 + core) * Q, 3 * Q, Q, far)

        def land(self, name):
            copy, dst, size = self.moves[name]
            copy.wait_recv()
            region = self.ref.at[pl.ds(dst, size), core]
            self.swaps[name] = push(region, region, twin)

        def swapped(self, name):
            self.swaps[name].wait_recv()

        def step(self, i):
            if i < m - 2:
                self.land(i)
                self.start(i + 1)
            elif i == m - 2:
                self.land("near")
                self.start(i + 1)
                self.land("far")
            else:
                self.land("last")

    def project(mat, base, size):
        @pl.loop(0, size)
        def _(k):
            q = base + k
            load(mat, q).wait()
            pacc[mat] += contract_cols(grads[mat, q], basis[mat, q].reshape(rank, cols))

    gathers = [Gather(basis.at[mat]) for mat in range(2)]
    for mat in range(2):
        gathers[mat].start(0)
    for mat in range(2):
        project(mat, 0, 1)
    for i in range(m):
        for mat in range(2):
            gathers[mat].step(i)
        if 1 <= i <= m - 2:
            for mat in range(2):
                gathers[mat].swapped(i - 1)
                project(mat, 2 ** (i - 1), 2 ** (i - 1))
    pt_copy = []
    for mat in range(2):
        for name in ("near", "far", "last"):
            gathers[mat].swapped(name)
        project(mat, Q, 3 * Q)
        ptsend[mat] = pacc[mat].T
        pt_copy.append(push(ptsend.at[mat], ptrecv.at[mat], twin))

    grams = [[], []]

    def round_product(mat):
        pt_copy[mat].wait_recv()
        prt_ref[mat] = ((ptsend[mat] + ptrecv[mat]) / pods).astype(jnp.bfloat16)
        gsend[mat, 0] = contract_cols(prt_ref[mat], prt_ref[mat])

    def gram_tasks():
        for k in range(m):
            target = {"row": me + delta[m - 1 - k]}
            copies = [push(gsend.at[mat, k], grecv.at[mat, k], target) for mat in range(2)]
            yield
            for mat in range(2):
                copies[mat].wait_recv()
                gsend[mat, k + 1] = gsend[mat, k] + grecv[mat, k]
        sub = lax.broadcasted_iota(jnp.int32, (rank, 2 * rank), 0)
        lane = lax.broadcasted_iota(jnp.int32, (rank, 2 * rank), 1)
        unit = jnp.where(lane == sub + rank, 1.0, 0.0).astype(jnp.float32)[:, rank:]
        systems = [jnp.concatenate([gsend[mat, m], unit], axis=1) for mat in range(2)]
        for k in range(rank):
            for mat in range(2):
                system = systems[mat]
                scale = 1.0 / jnp.sqrt(system[k : k + 1, k : k + 1])
                row = system[k : k + 1, :] * scale
                column = system[:, k : k + 1] * scale
                systems[mat] = jnp.where(
                    sub == k, row, jnp.where(sub > k, system - column * row, system)
                )
            if k % 8 == 7 and k < rank - 1:
                yield
        for mat in range(2):
            linv_ref[mat] = systems[mat][:, rank:]

    core_copy = [{}, {}]
    moved = [{}, {}]

    def multiply(mat, group):
        @pl.loop(group * Q, (group + 1) * Q)
        def _(q):
            product = jnp.dot(
                prt_ref[mat], grads[mat, q], preferred_element_type=jnp.float32
            )
            low, high = product[:half], product[half:]
            acc[mat, q] = jnp.where(core == 0, low, high)
            csend[mat, q] = jnp.where(core == 0, high, low).astype(jnp.bfloat16)

        region = pl.ds(group * Q, Q)
        core_copy[mat][group] = push(csend.at[mat, region], crecv.at[mat, region], twin)

    def add_core(mat, group):
        core_copy[mat][group].wait_recv()
        region = pl.ds(group * Q, Q)
        acc[mat, region] += crecv[mat, region].astype(jnp.float32)

    def reduce_send(mat, name, base, size, place, target):
        spot = pl.ds(place, size)
        rsend[mat, spot] = acc[mat, pl.ds(base, size)].astype(jnp.bfloat16)
        moved[mat][name] = (
            push(rsend.at[mat, spot], rrecv.at[mat, spot], target), place, size,
        )

    def reduce_add(mat, name, base):
        copy, place, size = moved[mat][name]
        copy.wait_recv()
        acc[mat, pl.ds(base, size)] += rrecv[mat, pl.ds(place, size)].astype(jnp.float32)

    def product_tasks(mat):
        multiply(mat, 3)
        yield
        multiply(mat, 2)
        yield
        add_core(mat, 3)
        reduce_send(mat, "second", 3 * Q, Q, Q, far)
        multiply(mat, 1)
        yield
        multiply(mat, 0)
        add_core(mat, 2)
        add_core(mat, 1)
        reduce_send(mat, "first", (2 - core) * Q, Q, 0, far)
        yield

    def reduce_tasks(mat):
        reduce_add(mat, "second", (1 + core) * Q)
        reduce_send(mat, "near", (1 + core) * Q, Q, 2 * Q, near)
        yield
        add_core(mat, 0)
        reduce_add(mat, "first", 0)
        yield
        reduce_add(mat, "near", 0)
        for i in reversed(range(m - 2)):
            reduce_send(mat, i, 2**i, 2**i, 3 * Q + Q - 2 ** (i + 1), partner[i])
            yield
            reduce_add(mat, i, 0)
        mine = acc[mat, 0] / pods
        own[mat, core] = mine
        sfull[mat, 0, core] = mine.astype(jnp.bfloat16)
        gather = Gather(sfull.at[mat])
        gather.start(0)
        own_copy = push(own.at[mat, core], own.at[mat, core], twin)
        region = sfull.at[mat, pl.ds(0, 1), core]
        gather.swaps["own"] = push(region, region, twin)
        yield
        for i in range(m):
            gather.step(i)
            yield
        own_copy.wait_recv()
        own_ref[mat] = own[mat].reshape(rank, cols)
        for name in gather.swaps:
            gather.swapped(name)

        for q in range(n):
            pltpu.make_async_copy(
                sfull.at[mat, q], out_refs[mat].at[block_of(q)], out_sems.at[mat * n + q]
            ).start()
        yield

    def drive(tasks, first_only=False):
        live = list(tasks)
        while live:
            for task in list(live):
                if next(task, StopIteration) is StopIteration:
                    live.remove(task)
                    if first_only and task is tasks[0]:
                        return

    round_product(0)
    gate_product = product_tasks(0)
    next(gate_product)
    next(gate_product)
    round_product(1)
    gram = gram_tasks()
    next(gram)
    drive([gate_product])
    gate_reduce = reduce_tasks(0)
    up_reduce = reduce_tasks(1)
    drive([product_tasks(1), gate_reduce, gram], first_only=True)
    drive([gate_reduce, up_reduce, gram])
    for mat in range(2):
        for q in range(n):
            pltpu.make_async_copy(
                sfull.at[mat, q], out_refs[mat].at[block_of(q)], out_sems.at[mat * n + q]
            ).wait()
    for copy in sent:
        copy.wait_send()


def copies_of(n):
    m = n.bit_length() - 1
    gather = 2 * (m + 1)
    return 2 * (gather + 1 + m + 4 + (m + 1) + gather + 2)


def residual_kernel(
    g0_ref, g1_ref, s0_ref, s1_ref, prt_ref, linv_ref, own_ref,
    next0_ref, next1_ref, factor0_ref, factor1_ref, r0_ref, r1_ref, left,
):
    @pl.when(pl.program_id(0) == 0)
    def _():
        for mat, (next_ref, factor_ref) in enumerate(
            ((next0_ref, factor0_ref), (next1_ref, factor1_ref))
        ):
            inverse = linv_ref[mat]
            next_ref[...] = jnp.dot(inverse, own_ref[mat], precision=HIGHEST)
            columns = jnp.dot(inverse, prt_ref[mat].astype(jnp.float32), precision=HIGHEST)
            factor = columns.T
            factor_ref[...] = factor
            mixed = jnp.dot(factor, inverse, precision=HIGHEST)
            top = mixed.astype(jnp.bfloat16)
            rest = (mixed - top.astype(jnp.float32)).astype(jnp.bfloat16)
            left[mat] = jnp.concatenate([top, rest], axis=1)

    for mat, (g_ref, s_ref, r_ref) in enumerate(
        ((g0_ref, s0_ref, r0_ref), (g1_ref, s1_ref, r1_ref))
    ):
        rank = prt_ref.shape[1]
        block = s_ref[0].reshape(rank, s_ref.shape[3])
        both = jnp.concatenate([block, block], axis=0)
        product = jnp.dot(left[mat], both, preferred_element_type=jnp.float32)
        r_ref[0] = (g_ref[0].astype(jnp.float32) - product).astype(jnp.bfloat16)


def fused(n, pods, grad_gate, grad_up, basis_gate, basis_up):
    _, rows, full_cols = grad_gate.shape
    rank, cols = basis_gate.shape
    half = rank // 2
    m = n.bit_length() - 1
    vmem = pl.BlockSpec(memory_space=pltpu.VMEM)
    anywhere = pl.BlockSpec(memory_space=pl.ANY)
    f32, bf16 = jnp.float32, jnp.bfloat16
    count = copies_of(n)
    s_gate, s_up, prt, linv, own = pl.pallas_call(
        functools.partial(gather_kernel, n, pods),
        out_shape=[
            jax.ShapeDtypeStruct((n, 2, half, cols), bf16),
            jax.ShapeDtypeStruct((n, 2, half, cols), bf16),
            jax.ShapeDtypeStruct((2, rank, rows), bf16),
            jax.ShapeDtypeStruct((2, rank, rank), f32),
            jax.ShapeDtypeStruct((2, rank, cols), f32),
        ],
        in_specs=[anywhere, anywhere, vmem, vmem],
        out_specs=[anywhere, anywhere, vmem, vmem, vmem],
        scratch_shapes=[
            pltpu.VMEM((2, n, rows, cols), bf16),
            pltpu.VMEM((2, n, 2, half, cols), bf16),
            pltpu.VMEM((2, n, 2, half, cols), bf16),
            pltpu.VMEM((2, n, half, cols), f32),
            pltpu.VMEM((2, n, half, cols), bf16),
            pltpu.VMEM((2, n, half, cols), bf16),
            pltpu.VMEM((2, n, half, cols), bf16),
            pltpu.VMEM((2, n, half, cols), bf16),
            pltpu.VMEM((2, rows, rank), f32),
            pltpu.VMEM((2, rank, rows), f32),
            pltpu.VMEM((2, rank, rows), f32),
            pltpu.VMEM((2, m + 1, rank, rank), f32),
            pltpu.VMEM((2, m, rank, rank), f32),
            pltpu.VMEM((2, 2, half, cols), f32),
            pltpu.SemaphoreType.DMA((count,)),
            pltpu.SemaphoreType.DMA((count,)),
            pltpu.SemaphoreType.DMA((2 * n,)),
            pltpu.SemaphoreType.DMA((2 * n,)),
        ],
        compiler_params=pltpu.CompilerParams(
            collective_id=0, has_side_effects=True, vmem_limit_bytes=56 * 2**20
        ),
        cost_estimate=pl.CostEstimate(
            flops=8 * rows * full_cols * rank,
            bytes_accessed=4 * rows * full_cols,
            transcendentals=0,
        ),
    )(grad_gate, grad_up, basis_gate, basis_up)

    def whole(array):
        return pl.BlockSpec(array.shape, lambda i: (0,) * array.ndim)

    def fixed(*shape):
        return pl.BlockSpec(shape, lambda i: (0,) * len(shape))

    block = pl.BlockSpec((1, rows, cols), lambda i: (0, 0, i))
    right = pl.BlockSpec((1, 2, half, cols), lambda i: (i, 0, 0, 0))
    return tuple(
        pl.pallas_call(
            residual_kernel,
            grid=(n,),
            out_shape=[
                jax.ShapeDtypeStruct((rank, cols), f32),
                jax.ShapeDtypeStruct((rank, cols), f32),
                jax.ShapeDtypeStruct((rows, rank), f32),
                jax.ShapeDtypeStruct((rows, rank), f32),
                jax.ShapeDtypeStruct(grad_gate.shape, bf16),
                jax.ShapeDtypeStruct(grad_up.shape, bf16),
            ],
            in_specs=[block, block, right, right, whole(prt), whole(linv), whole(own)],
            out_specs=[
                fixed(rank, cols), fixed(rank, cols), fixed(rows, rank), fixed(rows, rank),
                block, block,
            ],
            scratch_shapes=[pltpu.VMEM((2, rows, 2 * rank), bf16)],
            compiler_params=pltpu.CompilerParams(vmem_limit_bytes=48 * 2**20),
            cost_estimate=pl.CostEstimate(
                flops=4 * rows * full_cols * rank,
                bytes_accessed=8 * rows * full_cols,
                transcendentals=0,
            ),
        )(grad_gate, grad_up, s_gate, s_up, prt, linv, own)
    )


def dispatch(grad_gate, grad_up, basis_gate, basis_up):
    n = lax.axis_size("row")
    pods = lax.axis_size("outer")
    pod_part, rows, full_cols = grad_gate.shape
    rank, cols = basis_gate.shape
    fits = (
        pods == 2 and pod_part == 1 and n >= 4 and n & (n - 1) == 0
        and cols % 128 == 0 and rows % 128 == 0 and rank % 32 == 0
        and 4 * rows * full_cols <= 36 * 2**20
    )
    if fits:
        return fused(n, pods, grad_gate, grad_up, basis_gate, basis_up)
    return local(grad_gate, grad_up, basis_gate, basis_up)


def solution(mesh):
    return jax.shard_map(
        dispatch,
        mesh=mesh,
        in_specs=(P("outer", "row", None), P("outer", "row", None), P(None, "row"), P(None, "row")),
        out_specs=(
            P(None, "row"),
            P(None, "row"),
            P("row", None),
            P("row", None),
            P("outer", "row", None),
            P("outer", "row", None),
        ),
        check_vma=False,
    )
```

```python
import functools

import jax
import jax.numpy as jnp
from jax import lax
from jax.experimental import pallas as pl
from jax.experimental.pallas import tpu as pltpu
from jax.sharding import PartitionSpec as P

MESH = pl.DeviceIdType.MESH
HIGHEST = lax.Precision.HIGHEST


def forward_solve(lower_matrix, right_hand):
    return jax.scipy.linalg.solve_triangular(lower_matrix, right_hand, lower=True)


def contract_cols(left, right):
    return lax.dot_general(
        left, right, (((1,), (1,)), ((), ())), preferred_element_type=jnp.float32
    )


def contract_rows(left, right):
    return lax.dot_general(
        left, right, (((0,), (0,)), ((), ())), preferred_element_type=jnp.float32
    )


def local(grad_gate, grad_up, basis_gate, basis_up):
    pod_count = lax.axis_size("outer")
    gate_rows = grad_gate[0]
    up_rows = grad_up[0]
    full_cols = gate_rows.shape[1]
    summed = lax.psum(
        (
            contract_cols(gate_rows, lax.all_gather(basis_gate, "row", axis=1, tiled=True)),
            contract_cols(up_rows, lax.all_gather(basis_up, "row", axis=1, tiled=True)),
        ),
        "outer",
    )
    round_gate = (summed[0] / pod_count).astype(jnp.bfloat16)
    round_up = (summed[1] / pod_count).astype(jnp.bfloat16)
    gram_pair = lax.psum(
        (contract_rows(round_gate, round_gate), contract_rows(round_up, round_up)), "row"
    )
    lower_gate = jnp.linalg.cholesky(gram_pair[0])
    lower_up = jnp.linalg.cholesky(gram_pair[1])
    products = (contract_rows(round_gate, gate_rows), contract_rows(round_up, up_rows))
    shard_cols = full_cols // lax.axis_size("row")
    shard_start = lax.axis_index("row") * shard_cols
    totals = lax.psum((products[0], products[1]), ("outer", "row"))
    full_gate = forward_solve(lower_gate, totals[0] / pod_count)
    full_up = forward_solve(lower_up, totals[1] / pod_count)
    next_gate = lax.dynamic_slice_in_dim(full_gate, shard_start, shard_cols, 1)
    next_up = lax.dynamic_slice_in_dim(full_up, shard_start, shard_cols, 1)
    factor_gate = forward_solve(lower_gate, round_gate.astype(jnp.float32).T).T
    factor_up = forward_solve(lower_up, round_up.astype(jnp.float32).T).T
    resid_gate = (
        gate_rows - jnp.dot(factor_gate, full_gate, precision=lax.Precision.HIGHEST)
    ).astype(jnp.bfloat16)
    resid_up = (up_rows - jnp.dot(factor_up, full_up, precision=lax.Precision.HIGHEST)).astype(
        jnp.bfloat16
    )
    return (next_gate, next_up, factor_gate, factor_up, resid_gate[None], resid_up[None])


class Place:
    def __init__(self, n, send_sems, recv_sems):
        self.m = n.bit_length() - 1
        self.Q = n // 4
        self.me = lax.axis_index("row")
        self.core = lax.axis_index("outer")
        m = self.m
        delta = [(1 - 2 * ((self.me // 2**b) % 2)) * 2**b for b in range(m)]
        self.delta = delta
        self.slot_delta = [delta[m - 1 - i] for i in range(m - 2)] + [delta[0], delta[1]]
        self.near = {"row": self.me + (1 - self.core) * delta[0] + self.core * delta[1]}
        self.far = {"row": self.me + (1 - self.core) * delta[1] + self.core * delta[0]}
        self.partner = [{"row": self.me + delta[m - 1 - i]} for i in range(m - 2)]
        self.twin = {"outer": 1 - self.core}
        self.sems = (send_sems, recv_sems)
        self.sent = []

    def block_of(self, q):
        place = self.me
        for i in range(self.m):
            place = place + ((q // 2**i) % 2) * self.slot_delta[i]
        return place

    def greet(self):
        barrier = pltpu.get_barrier_semaphore()
        targets = self.partner + [
            {"row": self.me + self.delta[0]}, {"row": self.me + self.delta[1]}, self.twin,
        ]
        for target in targets:
            pl.semaphore_signal(barrier, inc=1, device_id=target, device_id_type=MESH)
        return lambda: pl.semaphore_wait(barrier, len(targets))

    def push(self, src, dst, target):
        i = len(self.sent)
        copy = pltpu.make_async_remote_copy(
            src_ref=src, dst_ref=dst, send_sem=self.sems[0].at[i], recv_sem=self.sems[1].at[i],
            device_id=target, device_id_type=MESH,
        )
        copy.start()
        self.sent.append(copy)
        return copy


class Gather:
    def __init__(self, place, ref):
        self.at = place
        self.ref = ref
        self.moves = {}
        self.swaps = {}

    def go(self, name, src, dst, size, target):
        core = self.at.core
        copy = self.at.push(
            self.ref.at[pl.ds(src, size), core], self.ref.at[pl.ds(dst, size), core], target
        )
        self.moves[name] = (copy, dst, size)

    def start(self, i):
        m, Q, core = self.at.m, self.at.Q, self.at.core
        if i < m - 2:
            self.go(i, 0, 2**i, 2**i, self.at.partner[i])
        elif i == m - 2:
            self.go("near", 0, (1 + core) * Q, Q, self.at.near)
            self.go("far", 0, (2 - core) * Q, Q, self.at.far)
        else:
            self.go("last", (1 + core) * Q, 3 * Q, Q, self.at.far)

    def land(self, name):
        copy, dst, size = self.moves[name]
        copy.wait_recv()
        self.swap(name, dst, size)

    def swap(self, name, dst, size):
        region = self.ref.at[pl.ds(dst, size), self.at.core]
        self.swaps[name] = self.at.push(region, region, self.at.twin)

    def swapped(self, name):
        self.swaps[name].wait_recv()

    def step(self, i):
        m = self.at.m
        if i < m - 2:
            self.land(i)
            self.start(i + 1)
        elif i == m - 2:
            self.land("near")
            self.start(i + 1)
            self.land("far")
        else:
            self.land("last")


def forward_kernel(
    n, pods, g0_ref, g1_ref, b0_ref, b1_ref, grads,
    prt_ref, basis, pacc, ptsend, ptrecv, sfull, acc, csend, crecv, rsend, rrecv, gsend, grecv, own,
    send_sems, recv_sems, g_sems,
):
    at = Place(n, send_sems, recv_sems)
    copies = project_part(
        at, n, g0_ref, g1_ref, b0_ref, b1_ref, grads, basis, pacc, ptsend, ptrecv, g_sems,
    )

    def round_product(mat):
        copies[mat].wait_recv()
        prt_ref[mat] = ((ptsend[mat] + ptrecv[mat]) / pods).astype(jnp.bfloat16)
        rows, rank = prt_ref.shape[2], prt_ref.shape[1]
        grads[mat, rows + rank :, :rows] = prt_ref[mat]
        gsend[mat, 0] = contract_cols(prt_ref[mat], prt_ref[mat])

    reduce_part(
        at, n, pods, b0_ref.shape[1], round_product, grads, prt_ref,
        sfull, acc, csend, crecv, rsend, rrecv, gsend, grecv, own,
    )
    for copy in at.sent:
        copy.wait_send()


def pack_of(rank, rows, cols):
    return rows + rank, rows, rows + 3 * cols


def terms(value):
    top = value.astype(jnp.bfloat16)
    rest = value - top.astype(jnp.float32)
    middle = rest.astype(jnp.bfloat16)
    return top, middle, (rest - middle.astype(jnp.float32)).astype(jnp.bfloat16)


def project_part(
    at, n, g0_ref, g1_ref, b0_ref, b1_ref, grads, basis, pacc, ptsend, ptrecv, g_sems,
):
    m, Q = at.m, at.Q
    rank, cols = b0_ref.shape
    grad_refs = (g0_ref, g1_ref)
    basis_refs = (b0_ref, b1_ref)

    def columns(q):
        return pl.ds(pl.multiple_of(at.block_of(q) * cols, 128), cols)

    def load(mat, q):
        return pltpu.make_async_copy(
            grad_refs[mat].at[0, :, columns(q)], grads.at[mat, pl.ds(0, grad_refs[mat].shape[1]), columns(q)],
            g_sems.at[mat * n + q],
        )

    greeted = at.greet()
    for mat in range(2):
        @pl.loop(0, n)
        def _(q):
            load(mat, q).start()

        basis[mat, 0] = basis_refs[mat][...].reshape(2, rank // 2, cols)
        pacc[mat] = jnp.zeros(pacc.shape[1:], jnp.float32)
    greeted()

    def project(mat, base, size):
        @pl.loop(0, size)
        def _(k):
            q = base + k
            load(mat, q).wait()
            pacc[mat] += contract_cols(
                grads[mat, pl.ds(0, grad_refs[mat].shape[1]), columns(q)], basis[mat, q].reshape(rank, cols)
            )

    gathers = [Gather(at, basis.at[mat]) for mat in range(2)]
    for mat in range(2):
        gathers[mat].start(0)
    for mat in range(2):
        project(mat, 0, 1)
    for i in range(m):
        for mat in range(2):
            gathers[mat].step(i)
        if 1 <= i <= m - 2:
            for mat in range(2):
                gathers[mat].swapped(i - 1)
                project(mat, 2 ** (i - 1), 2 ** (i - 1))
    copies = []
    for mat in range(2):
        for name in ("near", "far", "last"):
            gathers[mat].swapped(name)
        project(mat, Q, 3 * Q)
        ptsend[mat] = pacc[mat].T
        copies.append(at.push(ptsend.at[mat], ptrecv.at[mat], at.twin))
    return copies


def reduce_part(
    at, n, pods, cols, round_product, grads, prt_ref,
    sfull, acc, csend, crecv, rsend, rrecv, gsend, grecv, own,
):
    m, Q, core, near, far = at.m, at.Q, at.core, at.near, at.far
    rank, rows = prt_ref.shape[1:]
    half = rank // 2
    row_spot, own_spot, linv_spot = pack_of(rank, rows, cols)

    def columns(q):
        return pl.ds(pl.multiple_of(at.block_of(q) * cols, 128), cols)

    def gram_tasks():
        for k in range(m):
            target = {"row": at.me + at.delta[m - 1 - k]}
            copies = [at.push(gsend.at[mat, k], grecv.at[mat, k], target) for mat in range(2)]
            yield
            for mat in range(2):
                copies[mat].wait_recv()
                gsend[mat, k + 1] = gsend[mat, k] + grecv[mat, k]
        sub = lax.broadcasted_iota(jnp.int32, (rank, 2 * rank), 0)
        lane = lax.broadcasted_iota(jnp.int32, (rank, 2 * rank), 1)
        unit = jnp.where(lane == sub + rank, 1.0, 0.0).astype(jnp.float32)[:, rank:]
        systems = [jnp.concatenate([gsend[mat, m], unit], axis=1) for mat in range(2)]
        for k in range(rank):
            for mat in range(2):
                system = systems[mat]
                scale = 1.0 / jnp.sqrt(system[k : k + 1, k : k + 1])
                row = system[k : k + 1, :] * scale
                column = system[:, k : k + 1] * scale
                systems[mat] = jnp.where(
                    sub == k, row, jnp.where(sub > k, system - column * row, system)
                )
            if k % 8 == 7 and k < rank - 1:
                yield
        for mat in range(2):
            for part, value in enumerate(terms(systems[mat][:, rank:])):
                start = linv_spot + part * 128
                grads[mat, row_spot:, start : start + rank] = value

    core_copy = [{}, {}]
    moved = [{}, {}]

    def multiply(mat, group):
        @pl.loop(group * Q, (group + 1) * Q)
        def _(q):
            product = jnp.dot(
                prt_ref[mat], grads[mat, pl.ds(0, rows), columns(q)], preferred_element_type=jnp.float32
            )
            low, high = product[:half], product[half:]
            acc[mat, q] = jnp.where(core == 0, low, high)
            csend[mat, q] = jnp.where(core == 0, high, low).astype(jnp.bfloat16)

        region = pl.ds(group * Q, Q)
        core_copy[mat][group] = at.push(csend.at[mat, region], crecv.at[mat, region], at.twin)

    def add_core(mat, group):
        core_copy[mat][group].wait_recv()
        region = pl.ds(group * Q, Q)
        acc[mat, region] += crecv[mat, region].astype(jnp.float32)

    def reduce_send(mat, name, base, size, place, target):
        spot = pl.ds(place, size)
        rsend[mat, spot] = acc[mat, pl.ds(base, size)].astype(jnp.bfloat16)
        copy = at.push(rsend.at[mat, spot], rrecv.at[mat, spot], target)
        moved[mat][name] = (copy, place, size)

    def reduce_add(mat, name, base):
        copy, place, size = moved[mat][name]
        copy.wait_recv()
        acc[mat, pl.ds(base, size)] += rrecv[mat, pl.ds(place, size)].astype(jnp.float32)

    def product_tasks(mat):
        multiply(mat, 3)
        yield
        multiply(mat, 2)
        yield
        add_core(mat, 3)
        reduce_send(mat, "second", 3 * Q, Q, Q, far)
        multiply(mat, 1)
        yield
        multiply(mat, 0)
        add_core(mat, 2)
        add_core(mat, 1)
        reduce_send(mat, "first", (2 - core) * Q, Q, 0, far)
        yield

    def reduce_tasks(mat):
        reduce_add(mat, "second", (1 + core) * Q)
        reduce_send(mat, "near", (1 + core) * Q, Q, 2 * Q, near)
        yield
        add_core(mat, 0)
        reduce_add(mat, "first", 0)
        yield
        reduce_add(mat, "near", 0)
        for i in reversed(range(m - 2)):
            reduce_send(mat, i, 2**i, 2**i, 3 * Q + Q - 2 ** (i + 1), at.partner[i])
            yield
            reduce_add(mat, i, 0)
        mine = acc[mat, 0] / pods
        own[mat, core] = mine
        sfull[mat, 0, core] = mine.astype(jnp.bfloat16)
        gather = Gather(at, sfull.at[mat])
        gather.start(0)
        own_copy = at.push(own.at[mat, core], own.at[mat, core], at.twin)
        gather.swap("own", 0, 1)
        yield
        for i in range(m):
            gather.step(i)
            yield
        own_copy.wait_recv()
        for part, value in enumerate(terms(own[mat].reshape(rank, cols))):
            start = own_spot + part * cols
            grads[mat, row_spot:, start : start + cols] = value
        for name in gather.swaps:
            gather.swapped(name)

        @pl.loop(0, n)
        def _(q):
            grads[mat, pl.ds(rows, rank), columns(q)] = sfull[mat, q].reshape(rank, cols)

        yield

    def drive(tasks, first_only=False):
        live = list(tasks)
        while live:
            for task in list(live):
                if next(task, StopIteration) is StopIteration:
                    live.remove(task)
                    if first_only and task is tasks[0]:
                        return

    round_product(0)
    gate_product = product_tasks(0)
    next(gate_product)
    next(gate_product)
    round_product(1)
    gram = gram_tasks()
    next(gram)
    drive([gate_product])
    gate_reduce = reduce_tasks(0)
    up_reduce = reduce_tasks(1)
    drive([product_tasks(1), gate_reduce, gram], first_only=True)
    drive([gate_reduce, up_reduce, gram])


def residual_kernel(
    width, rank, rows, cols, grads,
    next0_ref, next1_ref, factor0_ref, factor1_ref, r0_ref, r1_ref, left, made, sems,
):
    row_spot, own_spot, linv_spot = pack_of(rank, rows, cols)
    tile = 256 if width % 256 == 0 else 128
    steps = grads.shape[2] // width
    for mat, (next_ref, factor_ref) in enumerate(
        ((next0_ref, factor0_ref), (next1_ref, factor1_ref))
    ):
        def whole(start, size, step):
            parts = [
                grads[mat, row_spot:, start + k * step : start + k * step + size].astype(jnp.float32)
                for k in range(3)
            ]
            return parts[0] + (parts[1] + parts[2])

        inverse = whole(linv_spot, rank, 128)
        next_ref[...] = jnp.dot(inverse, whole(own_spot, cols, cols), precision=HIGHEST)
        product = grads[mat, row_spot:, :rows].astype(jnp.float32)
        rows_t = jnp.dot(inverse, product, precision=HIGHEST)
        factor_ref[...] = rows_t
        mixed = lax.dot_general(inverse, rows_t, (((0,), (0,)), ((), ())), precision=HIGHEST).T
        top = mixed.astype(jnp.bfloat16)
        rest = (mixed - top.astype(jnp.float32)).astype(jnp.bfloat16)
        left[mat] = jnp.concatenate([top, rest], axis=1)

    def store(mat, i):
        slot = i % 2
        start = pl.multiple_of(i * width, 128)
        return pltpu.make_async_copy(
            made.at[mat, slot], (r0_ref, r1_ref)[mat].at[0, :, pl.ds(start, width)],
            sems.at[mat, slot],
        )

    @pl.loop(0, steps)
    def _(i):
        for mat in range(2):
            @pl.when(i >= 2)
            def _():
                store(mat, i - 2).wait()

            for k in range(width // tile):
                here = pl.ds(pl.multiple_of(i * width + k * tile, 128), tile)
                block = grads[mat, rows : rows + rank, here]
                product = jnp.dot(
                    left[mat], jnp.concatenate([block, block], axis=0),
                    preferred_element_type=jnp.float32,
                )
                made[mat, i % 2, :, k * tile : (k + 1) * tile] = (
                    grads[mat, :rows, here].astype(jnp.float32) - product
                ).astype(jnp.bfloat16)
            store(mat, i).start()

    for i in range(max(steps - 2, 0), steps):
        for mat in range(2):
            store(mat, i).wait()


def fused(n, pods, grad_gate, grad_up, basis_gate, basis_up):
    _, rows, full_cols = grad_gate.shape
    rank, cols = basis_gate.shape
    half = rank // 2
    m = n.bit_length() - 1
    vmem = pl.BlockSpec(memory_space=pltpu.VMEM)
    anywhere = pl.BlockSpec(memory_space=pl.ANY)
    f32, bf16 = jnp.float32, jnp.bfloat16
    flops = 4 * rows * full_cols * rank

    gather = 2 * (m + 1)
    count = 2 * (gather + 1 + m + 4 + (m + 1) + gather + 2)
    packed = pl.pallas_call(
        functools.partial(forward_kernel, n, pods),
        out_shape=pltpu.VMEM((2, rows + 2 * rank, full_cols), bf16),
        in_specs=[anywhere, anywhere, vmem, vmem],
        out_specs=vmem,
        scratch_shapes=[
            pltpu.VMEM((2, rank, rows), bf16),
            pltpu.VMEM((2, n, 2, half, cols), bf16),
            pltpu.VMEM((2, rows, rank), f32),
            pltpu.VMEM((2, rank, rows), f32),
            pltpu.VMEM((2, rank, rows), f32),
            pltpu.VMEM((2, n, 2, half, cols), bf16),
            pltpu.VMEM((2, n, half, cols), f32),
            pltpu.VMEM((2, n, half, cols), bf16),
            pltpu.VMEM((2, n, half, cols), bf16),
            pltpu.VMEM((2, n, half, cols), bf16),
            pltpu.VMEM((2, n, half, cols), bf16),
            pltpu.VMEM((2, m + 1, rank, rank), f32),
            pltpu.VMEM((2, m, rank, rank), f32),
            pltpu.VMEM((2, 2, half, cols), f32),
            pltpu.SemaphoreType.DMA((count,)),
            pltpu.SemaphoreType.DMA((count,)),
            pltpu.SemaphoreType.DMA((2 * n,)),
        ],
        compiler_params=pltpu.CompilerParams(
            collective_id=0, has_side_effects=True, vmem_limit_bytes=20 * 2**20
        ),
        cost_estimate=pl.CostEstimate(
            flops=2 * flops, bytes_accessed=4 * rows * full_cols, transcendentals=0
        ),
    )(grad_gate, grad_up, basis_gate, basis_up)

    width = next(
        w for w in (1024, 512, 256, 128) if full_cols % w == 0
    )
    next_gate, next_up, factor_gate, factor_up, resid_gate, resid_up = pl.pallas_call(
        functools.partial(residual_kernel, width, rank, rows, cols),
        out_shape=[
            jax.ShapeDtypeStruct((rank, cols), f32),
            jax.ShapeDtypeStruct((rank, cols), f32),
            jax.ShapeDtypeStruct((rank, rows), f32),
            jax.ShapeDtypeStruct((rank, rows), f32),
            jax.ShapeDtypeStruct(grad_gate.shape, bf16),
            jax.ShapeDtypeStruct(grad_up.shape, bf16),
        ],
        in_specs=[vmem],
        out_specs=[vmem] * 4 + [anywhere] * 2,
        scratch_shapes=[
            pltpu.VMEM((2, rows, 2 * rank), bf16),
            pltpu.VMEM((2, 2, rows, width), bf16),
            pltpu.SemaphoreType.DMA((2, 2)),
        ],
        compiler_params=pltpu.CompilerParams(vmem_limit_bytes=20 * 2**20),
        cost_estimate=pl.CostEstimate(
            flops=flops, bytes_accessed=4 * rows * full_cols, transcendentals=0
        ),
    )(packed)
    return next_gate, next_up, factor_gate.T, factor_up.T, resid_gate, resid_up


def dispatch(grad_gate, grad_up, basis_gate, basis_up):
    n = lax.axis_size("row")
    pods = lax.axis_size("outer")
    pod_part, rows, full_cols = grad_gate.shape
    rank, cols = basis_gate.shape
    fits = (
        pods == 2 and pod_part == 1 and n >= 4 and n & (n - 1) == 0
        and cols % 128 == 0 and rows % 128 == 0 and rank % 32 == 0
        and 4 * rows * full_cols <= 32 * 2**20 and rows + 3 * cols + 384 <= full_cols
        and rank <= 128
    )
    if fits:
        return fused(n, pods, grad_gate, grad_up, basis_gate, basis_up)
    return local(grad_gate, grad_up, basis_gate, basis_up)


def solution(mesh):
    return jax.shard_map(
        dispatch,
        mesh=mesh,
        in_specs=(P("outer", "row", None), P("outer", "row", None), P(None, "row"), P(None, "row")),
        out_specs=(
            P(None, "row"),
            P(None, "row"),
            P("row", None),
            P("row", None),
            P("outer", "row", None),
            P("outer", "row", None),
        ),
        check_vma=False,
    )
```

```python
import functools

import jax
import jax.numpy as jnp
from jax import lax
from jax.experimental import pallas as pl
from jax.experimental.pallas import tpu as pltpu
from jax.sharding import PartitionSpec as P

MESH = pl.DeviceIdType.MESH
HIGHEST = lax.Precision.HIGHEST


def forward_solve(lower_matrix, right_hand):
    return jax.scipy.linalg.solve_triangular(lower_matrix, right_hand, lower=True)


def contract_cols(left, right):
    return lax.dot_general(
        left, right, (((1,), (1,)), ((), ())), preferred_element_type=jnp.float32
    )


def contract_rows(left, right):
    return lax.dot_general(
        left, right, (((0,), (0,)), ((), ())), preferred_element_type=jnp.float32
    )


def local(grad_gate, grad_up, basis_gate, basis_up):
    pod_count = lax.axis_size("outer")
    gate_rows = grad_gate[0]
    up_rows = grad_up[0]
    full_cols = gate_rows.shape[1]
    summed = lax.psum(
        (
            contract_cols(gate_rows, lax.all_gather(basis_gate, "row", axis=1, tiled=True)),
            contract_cols(up_rows, lax.all_gather(basis_up, "row", axis=1, tiled=True)),
        ),
        "outer",
    )
    round_gate = (summed[0] / pod_count).astype(jnp.bfloat16)
    round_up = (summed[1] / pod_count).astype(jnp.bfloat16)
    gram_pair = lax.psum(
        (contract_rows(round_gate, round_gate), contract_rows(round_up, round_up)), "row"
    )
    lower_gate = jnp.linalg.cholesky(gram_pair[0])
    lower_up = jnp.linalg.cholesky(gram_pair[1])
    products = (contract_rows(round_gate, gate_rows), contract_rows(round_up, up_rows))
    shard_cols = full_cols // lax.axis_size("row")
    shard_start = lax.axis_index("row") * shard_cols
    totals = lax.psum((products[0], products[1]), ("outer", "row"))
    full_gate = forward_solve(lower_gate, totals[0] / pod_count)
    full_up = forward_solve(lower_up, totals[1] / pod_count)
    next_gate = lax.dynamic_slice_in_dim(full_gate, shard_start, shard_cols, 1)
    next_up = lax.dynamic_slice_in_dim(full_up, shard_start, shard_cols, 1)
    factor_gate = forward_solve(lower_gate, round_gate.astype(jnp.float32).T).T
    factor_up = forward_solve(lower_up, round_up.astype(jnp.float32).T).T
    resid_gate = (
        gate_rows - jnp.dot(factor_gate, full_gate, precision=lax.Precision.HIGHEST)
    ).astype(jnp.bfloat16)
    resid_up = (up_rows - jnp.dot(factor_up, full_up, precision=lax.Precision.HIGHEST)).astype(
        jnp.bfloat16
    )
    return (next_gate, next_up, factor_gate, factor_up, resid_gate[None], resid_up[None])


class Place:
    def __init__(self, n, send_sems, recv_sems):
        self.m = n.bit_length() - 1
        self.Q = n // 4
        self.me = lax.axis_index("row")
        self.core = lax.axis_index("outer")
        m = self.m
        delta = [(1 - 2 * ((self.me // 2**b) % 2)) * 2**b for b in range(m)]
        self.delta = delta
        self.slot_delta = [delta[m - 1 - i] for i in range(m - 2)] + [delta[0], delta[1]]
        self.near = {"row": self.me + (1 - self.core) * delta[0] + self.core * delta[1]}
        self.far = {"row": self.me + (1 - self.core) * delta[1] + self.core * delta[0]}
        self.peers = [
            {"row": self.me + sum(((p // 2**i) % 2) * delta[m - 1 - i] for i in range(m - 2))}
            for p in range(self.Q)
        ]
        self.twin = {"outer": 1 - self.core}
        self.sems = (send_sems, recv_sems)
        self.sent = []

    def block_of(self, q):
        place = self.me
        for i in range(self.m):
            place = place + ((q // 2**i) % 2) * self.slot_delta[i]
        return place

    def greet(self):
        barrier = pltpu.get_barrier_semaphore()
        targets = self.peers[1:] + [
            {"row": self.me + self.delta[0]}, {"row": self.me + self.delta[1]}, self.twin,
        ]
        for target in targets:
            pl.semaphore_signal(barrier, inc=1, device_id=target, device_id_type=MESH)
        return lambda: pl.semaphore_wait(barrier, len(targets))

    def push(self, src, dst, target):
        i = len(self.sent)
        copy = pltpu.make_async_remote_copy(
            src_ref=src, dst_ref=dst, send_sem=self.sems[0].at[i], recv_sem=self.sems[1].at[i],
            device_id=target, device_id_type=MESH,
        )
        copy.start()
        self.sent.append(copy)
        return copy


class Gather:
    def __init__(self, place, ref):
        self.at = place
        self.ref = ref
        self.moves = {}
        self.swaps = {}

    def go(self, name, src, dst, size, target):
        core = self.at.core
        copy = self.at.push(
            self.ref.at[pl.ds(src, size), core], self.ref.at[pl.ds(dst, size), core], target
        )
        self.moves[name] = (copy, dst, size)

    def start(self):
        for p in range(1, self.at.Q):
            self.go(p, 0, p, 1, self.at.peers[p])

    def spread(self):
        Q, core = self.at.Q, self.at.core
        for p in range(1, Q):
            self.moves[p][0].wait_recv()
        self.go("near", 0, (1 + core) * Q, Q, self.at.near)
        self.go("far", 0, (2 - core) * Q, Q, self.at.far)
        self.swap("peers", 1, Q - 1)

    def pass_on(self):
        Q, core = self.at.Q, self.at.core
        self.moves["near"][0].wait_recv()
        self.go("last", (1 + core) * Q, 3 * Q, Q, self.at.far)
        self.land("near")
        self.land("far")

    def land(self, name):
        copy, dst, size = self.moves[name]
        if name != "near":
            copy.wait_recv()
        self.swap(name, dst, size)

    def swap(self, name, dst, size):
        region = self.ref.at[pl.ds(dst, size), self.at.core]
        self.swaps[name] = self.at.push(region, region, self.at.twin)

    def swapped(self, *names):
        for name in names:
            self.swaps[name].wait_recv()


def forward_kernel(
    n, pods, g0_ref, g1_ref, b0_ref, b1_ref, grads,
    prt_ref, basis, pacc, ptsend, ptrecv, sfull, acc, csend, crecv, rsend, rrecv, gsend, grecv, own,
    send_sems, recv_sems, g_sems, b_sems,
):
    at = Place(n, send_sems, recv_sems)
    upper = project_part(
        at, n, g0_ref, g1_ref, b0_ref, b1_ref, grads, basis, pacc, ptsend, ptrecv, g_sems,
        b_sems,
    )
    copies = [next(upper)]

    def round_product(mat):
        copies[mat].wait_recv()
        prt_ref[mat] = ((ptsend[mat] + ptrecv[mat]) / pods).astype(jnp.bfloat16)
        rows, rank = prt_ref.shape[2], prt_ref.shape[1]
        grads[mat, rows + rank :, :rows] = prt_ref[mat]
        gsend[mat, 0] = contract_cols(prt_ref[mat], prt_ref[mat])

    reduce_part(
        at, n, pods, b0_ref.shape[1], upper, copies, round_product, grads, prt_ref,
        sfull, acc, csend, crecv, rsend, rrecv, gsend, grecv, own,
    )
    for copy in at.sent:
        copy.wait_send()


def pack_of(rank, rows, cols):
    return rows + rank, rows, rows + 3 * cols


def terms(value):
    top = value.astype(jnp.bfloat16)
    rest = value - top.astype(jnp.float32)
    middle = rest.astype(jnp.bfloat16)
    return top, middle, (rest - middle.astype(jnp.float32)).astype(jnp.bfloat16)


def project_part(
    at, n, g0_ref, g1_ref, b0_ref, b1_ref, grads, basis, pacc, ptsend, ptrecv, g_sems,
    b_sems,
):
    m, Q = at.m, at.Q
    rank, cols = b0_ref.shape
    grad_refs = (g0_ref, g1_ref)
    basis_refs = (b0_ref, b1_ref)

    def columns(q):
        return pl.ds(pl.multiple_of(at.block_of(q) * cols, 128), cols)

    def load(mat, q):
        return pltpu.make_async_copy(
            grad_refs[mat].at[0, :, columns(q)], grads.at[mat, pl.ds(0, grad_refs[mat].shape[1]), columns(q)],
            g_sems.at[mat * n + q],
        )

    greeted = at.greet()
    own = [
        pltpu.make_async_copy(
            basis_refs[mat].at[pl.ds(part * (rank // 2), rank // 2)], basis.at[mat, 0, part],
            b_sems.at[2 * mat + part],
        )
        for mat in range(2)
        for part in range(2)
    ]
    for copy in own:
        copy.start()
    for mat in range(2):
        @pl.loop(0, n)
        def _(q):
            load(mat, q).start()

        pacc[mat] = jnp.zeros(pacc.shape[1:], jnp.float32)
    for copy in own:
        copy.wait()
    greeted()

    def project(mat, base, size):
        @pl.loop(0, size)
        def _(k):
            q = base + k
            load(mat, q).wait()
            pacc[mat] += contract_cols(
                grads[mat, pl.ds(0, grad_refs[mat].shape[1]), columns(q)], basis[mat, q].reshape(rank, cols)
            )

    def exchange(mat):
        ptsend[mat] = pacc[mat].T
        return at.push(ptsend.at[mat], ptrecv.at[mat], at.twin)

    gate, up = (Gather(at, basis.at[mat]) for mat in range(2))
    gate.start()
    project(0, 0, 1)
    gate.spread()
    up.start()
    gate.swapped("peers")
    project(0, 1, Q - 1)
    project(1, 0, 1)
    gate.pass_on()
    up.spread()
    gate.swapped("near", "far")
    project(0, Q, 2 * Q)
    gate.land("last")
    up.swapped("peers")
    project(1, 1, Q - 1)
    gate.swapped("last")
    project(0, 3 * Q, Q)
    yield exchange(0)
    up.pass_on()
    yield
    up.land("last")
    up.swapped("near", "far")
    yield
    project(1, Q, 2 * Q)
    up.swapped("last")
    project(1, 3 * Q, Q)
    yield exchange(1)


def reduce_part(
    at, n, pods, cols, upper, copies, round_product, grads, prt_ref,
    sfull, acc, csend, crecv, rsend, rrecv, gsend, grecv, own,
):
    m, Q, core, near, far = at.m, at.Q, at.core, at.near, at.far
    rank, rows = prt_ref.shape[1:]
    half = rank // 2
    row_spot, own_spot, linv_spot = pack_of(rank, rows, cols)

    def columns(q):
        return pl.ds(pl.multiple_of(at.block_of(q) * cols, 128), cols)

    def gram_tasks():
        spot = 0
        for k, targets in enumerate(
            (at.peers[1:], [{"row": at.me + at.delta[1]}], [{"row": at.me + at.delta[0]}])
        ):
            moves = [
                [
                    at.push(gsend.at[mat, k], grecv.at[mat, spot + i], target)
                    for i, target in enumerate(targets)
                ]
                for mat in range(2)
            ]
            yield
            for mat in range(2):
                total = gsend[mat, k]
                for i, move in enumerate(moves[mat]):
                    move.wait_recv()
                    total = total + grecv[mat, spot + i]
                gsend[mat, k + 1] = total
            spot += len(targets)
        sub = lax.broadcasted_iota(jnp.int32, (rank, 2 * rank), 0)
        lane = lax.broadcasted_iota(jnp.int32, (rank, 2 * rank), 1)
        unit = jnp.where(lane == sub + rank, 1.0, 0.0).astype(jnp.float32)[:, rank:]
        systems = [jnp.concatenate([gsend[mat, 3], unit], axis=1) for mat in range(2)]
        for k in range(rank):
            for mat in range(2):
                system = systems[mat]
                scale = 1.0 / jnp.sqrt(system[k : k + 1, k : k + 1])
                row = system[k : k + 1, :] * scale
                column = system[:, k : k + 1] * scale
                systems[mat] = jnp.where(
                    sub == k, row, jnp.where(sub > k, system - column * row, system)
                )
            if k % 8 == 7 and k < rank - 1:
                yield
        for mat in range(2):
            for part, value in enumerate(terms(systems[mat][:, rank:])):
                start = linv_spot + part * 128
                grads[mat, row_spot:, start : start + rank] = value

    core_copy = [{}, {}]
    moved = [{}, {}]

    def multiply(mat, group):
        @pl.loop(group * Q, (group + 1) * Q)
        def _(q):
            product = jnp.dot(
                prt_ref[mat], grads[mat, pl.ds(0, rows), columns(q)], preferred_element_type=jnp.float32
            )
            low, high = product[:half], product[half:]
            acc[mat, q] = jnp.where(core == 0, low, high)
            csend[mat, q] = jnp.where(core == 0, high, low).astype(jnp.bfloat16)

        region = pl.ds(group * Q, Q)
        core_copy[mat][group] = at.push(csend.at[mat, region], crecv.at[mat, region], at.twin)

    def add_core(mat, group):
        core_copy[mat][group].wait_recv()
        region = pl.ds(group * Q, Q)
        acc[mat, region] += crecv[mat, region].astype(jnp.float32)

    def reduce_send(mat, name, base, size, place, target):
        spot = pl.ds(place, size)
        rsend[mat, spot] = acc[mat, pl.ds(base, size)].astype(jnp.bfloat16)
        copy = at.push(rsend.at[mat, spot], rrecv.at[mat, spot], target)
        moved[mat][name] = (copy, place, size)

    def reduce_add(mat, name, base):
        copy, place, size = moved[mat][name]
        copy.wait_recv()
        acc[mat, pl.ds(base, size)] += rrecv[mat, pl.ds(place, size)].astype(jnp.float32)

    def product_tasks(mat):
        multiply(mat, 3)
        yield
        multiply(mat, 2)
        yield
        add_core(mat, 3)
        reduce_send(mat, "second", 3 * Q, Q, Q, far)
        multiply(mat, 1)
        yield
        multiply(mat, 0)
        add_core(mat, 2)
        add_core(mat, 1)
        reduce_send(mat, "first", (2 - core) * Q, Q, 0, far)
        yield

    def reduce_tasks(mat):
        reduce_add(mat, "second", (1 + core) * Q)
        reduce_send(mat, "near", (1 + core) * Q, Q, 2 * Q, near)
        yield
        add_core(mat, 0)
        reduce_add(mat, "first", 0)
        yield
        reduce_add(mat, "near", 0)
        rsend[mat, pl.ds(3 * Q, Q - 1)] = acc[mat, pl.ds(1, Q - 1)].astype(jnp.bfloat16)
        for p in range(1, Q):
            spot = pl.ds(3 * Q + p - 1, 1)
            moved[mat][p] = (
                at.push(rsend.at[mat, spot], rrecv.at[mat, spot], at.peers[p]), 3 * Q + p - 1, 1,
            )
        yield
        for p in range(1, Q):
            reduce_add(mat, p, 0)
        mine = acc[mat, 0] / pods
        own[mat, core] = mine
        sfull[mat, 0, core] = mine.astype(jnp.bfloat16)
        gather = Gather(at, sfull.at[mat])
        gather.start()
        own_copy = at.push(own.at[mat, core], own.at[mat, core], at.twin)
        gather.swap("own", 0, 1)
        yield
        gather.spread()
        yield
        gather.pass_on()
        yield
        gather.land("last")
        yield
        own_copy.wait_recv()
        for part, value in enumerate(terms(own[mat].reshape(rank, cols))):
            start = own_spot + part * cols
            grads[mat, row_spot:, start : start + cols] = value
        gather.swapped(*gather.swaps)

        @pl.loop(0, n)
        def _(q):
            grads[mat, pl.ds(rows, rank), columns(q)] = sfull[mat, q].reshape(rank, cols)

        yield

    def drive(tasks, first_only=False):
        live = list(tasks)
        while live:
            for task in list(live):
                if next(task, StopIteration) is StopIteration:
                    live.remove(task)
                    if first_only and task is tasks[0]:
                        return

    round_product(0)
    gate_product = product_tasks(0)
    next(gate_product)
    next(upper)
    next(gate_product)
    next(gate_product)
    next(upper)
    next(gate_product)
    copies.append(next(upper))
    gate_reduce = reduce_tasks(0)
    next(gate_reduce)
    round_product(1)
    gram = gram_tasks()
    next(gram)
    up_reduce = reduce_tasks(1)
    drive([product_tasks(1), gate_reduce, gram], first_only=True)
    drive([gate_reduce, up_reduce, gram])


def residual_kernel(
    width, rank, rows, cols, grads,
    next0_ref, next1_ref, factor0_ref, factor1_ref, r0_ref, r1_ref, left, made, sems,
):
    row_spot, own_spot, linv_spot = pack_of(rank, rows, cols)
    tile = 256 if width % 256 == 0 else 128
    steps = grads.shape[2] // width
    for mat, (next_ref, factor_ref) in enumerate(
        ((next0_ref, factor0_ref), (next1_ref, factor1_ref))
    ):
        def whole(start, size, step):
            parts = [
                grads[mat, row_spot:, start + k * step : start + k * step + size].astype(jnp.float32)
                for k in range(3)
            ]
            return parts[0] + (parts[1] + parts[2])

        inverse = whole(linv_spot, rank, 128)
        next_ref[...] = jnp.dot(inverse, whole(own_spot, cols, cols), precision=HIGHEST)
        product = grads[mat, row_spot:, :rows].astype(jnp.float32)
        rows_t = jnp.dot(inverse, product, precision=HIGHEST)
        factor_ref[...] = rows_t
        mixed = lax.dot_general(inverse, rows_t, (((0,), (0,)), ((), ())), precision=HIGHEST).T
        top = mixed.astype(jnp.bfloat16)
        rest = (mixed - top.astype(jnp.float32)).astype(jnp.bfloat16)
        left[mat] = jnp.concatenate([top, rest], axis=1)

    def store(mat, i):
        slot = i % 2
        start = pl.multiple_of(i * width, 128)
        return pltpu.make_async_copy(
            made.at[mat, slot], (r0_ref, r1_ref)[mat].at[0, :, pl.ds(start, width)],
            sems.at[mat, slot],
        )

    @pl.loop(0, steps)
    def _(i):
        for mat in range(2):
            @pl.when(i >= 2)
            def _():
                store(mat, i - 2).wait()

            for k in range(width // tile):
                here = pl.ds(pl.multiple_of(i * width + k * tile, 128), tile)
                block = grads[mat, rows : rows + rank, here]
                product = jnp.dot(
                    left[mat], jnp.concatenate([block, block], axis=0),
                    preferred_element_type=jnp.float32,
                )
                made[mat, i % 2, :, k * tile : (k + 1) * tile] = (
                    grads[mat, :rows, here].astype(jnp.float32) - product
                ).astype(jnp.bfloat16)
            store(mat, i).start()

    for i in range(max(steps - 2, 0), steps):
        for mat in range(2):
            store(mat, i).wait()


def fused(n, pods, grad_gate, grad_up, basis_gate, basis_up):
    _, rows, full_cols = grad_gate.shape
    rank, cols = basis_gate.shape
    half = rank // 2
    vmem = pl.BlockSpec(memory_space=pltpu.VMEM)
    anywhere = pl.BlockSpec(memory_space=pl.ANY)
    hbm = pl.BlockSpec(memory_space=pltpu.HBM)
    f32, bf16 = jnp.float32, jnp.bfloat16
    flops = 4 * rows * full_cols * rank

    gather = (n // 4 - 1) + 3 + 4
    count = 2 * (gather + 1 + (n // 4 + 1) + 4 + (n // 4 + 2) + gather + 2)
    packed = pl.pallas_call(
        functools.partial(forward_kernel, n, pods),
        out_shape=pltpu.VMEM((2, rows + 2 * rank, full_cols), bf16),
        in_specs=[anywhere, anywhere, hbm, hbm],
        out_specs=vmem,
        scratch_shapes=[
            pltpu.VMEM((2, rank, rows), bf16),
            pltpu.VMEM((2, n, 2, half, cols), bf16),
            pltpu.VMEM((2, rows, rank), f32),
            pltpu.VMEM((2, rank, rows), f32),
            pltpu.VMEM((2, rank, rows), f32),
            pltpu.VMEM((2, n, 2, half, cols), bf16),
            pltpu.VMEM((2, n, half, cols), f32),
            pltpu.VMEM((2, n, half, cols), bf16),
            pltpu.VMEM((2, n, half, cols), bf16),
            pltpu.VMEM((2, n, half, cols), bf16),
            pltpu.VMEM((2, n, half, cols), bf16),
            pltpu.VMEM((2, 4, rank, rank), f32),
            pltpu.VMEM((2, n // 4 + 1, rank, rank), f32),
            pltpu.VMEM((2, 2, half, cols), f32),
            pltpu.SemaphoreType.DMA((count,)),
            pltpu.SemaphoreType.DMA((count,)),
            pltpu.SemaphoreType.DMA((2 * n,)),
            pltpu.SemaphoreType.DMA((4,)),
        ],
        compiler_params=pltpu.CompilerParams(
            collective_id=0, has_side_effects=True, vmem_limit_bytes=20 * 2**20
        ),
        cost_estimate=pl.CostEstimate(
            flops=2 * flops, bytes_accessed=4 * rows * full_cols, transcendentals=0
        ),
    )(grad_gate, grad_up, basis_gate, basis_up)

    width = next(
        w for w in (1024, 512, 256, 128) if full_cols % w == 0
    )
    next_gate, next_up, factor_gate, factor_up, resid_gate, resid_up = pl.pallas_call(
        functools.partial(residual_kernel, width, rank, rows, cols),
        out_shape=[
            jax.ShapeDtypeStruct((rank, cols), f32),
            jax.ShapeDtypeStruct((rank, cols), f32),
            jax.ShapeDtypeStruct((rank, rows), f32),
            jax.ShapeDtypeStruct((rank, rows), f32),
            jax.ShapeDtypeStruct(grad_gate.shape, bf16),
            jax.ShapeDtypeStruct(grad_up.shape, bf16),
        ],
        in_specs=[vmem],
        out_specs=[vmem] * 4 + [anywhere] * 2,
        scratch_shapes=[
            pltpu.VMEM((2, rows, 2 * rank), bf16),
            pltpu.VMEM((2, 2, rows, width), bf16),
            pltpu.SemaphoreType.DMA((2, 2)),
        ],
        compiler_params=pltpu.CompilerParams(vmem_limit_bytes=20 * 2**20),
        cost_estimate=pl.CostEstimate(
            flops=flops, bytes_accessed=4 * rows * full_cols, transcendentals=0
        ),
    )(packed)
    return next_gate, next_up, factor_gate.T, factor_up.T, resid_gate, resid_up


def dispatch(grad_gate, grad_up, basis_gate, basis_up):
    n = lax.axis_size("row")
    pods = lax.axis_size("outer")
    pod_part, rows, full_cols = grad_gate.shape
    rank, cols = basis_gate.shape
    fits = (
        pods == 2 and pod_part == 1 and n >= 4 and n & (n - 1) == 0
        and cols % 128 == 0 and rows % 128 == 0 and rank % 32 == 0
        and 4 * rows * full_cols <= 32 * 2**20 and rows + 3 * cols + 384 <= full_cols
        and rank <= 128
    )
    if fits:
        return fused(n, pods, grad_gate, grad_up, basis_gate, basis_up)
    return local(grad_gate, grad_up, basis_gate, basis_up)


def solution(mesh):
    return jax.shard_map(
        dispatch,
        mesh=mesh,
        in_specs=(P("outer", "row", None), P("outer", "row", None), P(None, "row"), P(None, "row")),
        out_specs=(
            P(None, "row"),
            P(None, "row"),
            P("row", None),
            P("row", None),
            P("outer", "row", None),
            P("outer", "row", None),
        ),
        check_vma=False,
    )
```

```python
import functools

import jax
import jax.numpy as jnp
from jax import lax
from jax.experimental import pallas as pl
from jax.experimental.pallas import tpu as pltpu
from jax.sharding import PartitionSpec as P

MESH = pl.DeviceIdType.MESH
HIGHEST = lax.Precision.HIGHEST


def forward_solve(lower_matrix, right_hand):
    return jax.scipy.linalg.solve_triangular(lower_matrix, right_hand, lower=True)


def contract_cols(left, right):
    return lax.dot_general(
        left, right, (((1,), (1,)), ((), ())), preferred_element_type=jnp.float32
    )


def contract_rows(left, right):
    return lax.dot_general(
        left, right, (((0,), (0,)), ((), ())), preferred_element_type=jnp.float32
    )


def local(grad_gate, grad_up, basis_gate, basis_up):
    pod_count = lax.axis_size("outer")
    gate_rows = grad_gate[0]
    up_rows = grad_up[0]
    full_cols = gate_rows.shape[1]
    summed = lax.psum(
        (
            contract_cols(gate_rows, lax.all_gather(basis_gate, "row", axis=1, tiled=True)),
            contract_cols(up_rows, lax.all_gather(basis_up, "row", axis=1, tiled=True)),
        ),
        "outer",
    )
    round_gate = (summed[0] / pod_count).astype(jnp.bfloat16)
    round_up = (summed[1] / pod_count).astype(jnp.bfloat16)
    gram_pair = lax.psum(
        (contract_rows(round_gate, round_gate), contract_rows(round_up, round_up)), "row"
    )
    lower_gate = jnp.linalg.cholesky(gram_pair[0])
    lower_up = jnp.linalg.cholesky(gram_pair[1])
    products = (contract_rows(round_gate, gate_rows), contract_rows(round_up, up_rows))
    shard_cols = full_cols // lax.axis_size("row")
    shard_start = lax.axis_index("row") * shard_cols
    totals = lax.psum((products[0], products[1]), ("outer", "row"))
    full_gate = forward_solve(lower_gate, totals[0] / pod_count)
    full_up = forward_solve(lower_up, totals[1] / pod_count)
    next_gate = lax.dynamic_slice_in_dim(full_gate, shard_start, shard_cols, 1)
    next_up = lax.dynamic_slice_in_dim(full_up, shard_start, shard_cols, 1)
    factor_gate = forward_solve(lower_gate, round_gate.astype(jnp.float32).T).T
    factor_up = forward_solve(lower_up, round_up.astype(jnp.float32).T).T
    resid_gate = (
        gate_rows - jnp.dot(factor_gate, full_gate, precision=lax.Precision.HIGHEST)
    ).astype(jnp.bfloat16)
    resid_up = (up_rows - jnp.dot(factor_up, full_up, precision=lax.Precision.HIGHEST)).astype(
        jnp.bfloat16
    )
    return (next_gate, next_up, factor_gate, factor_up, resid_gate[None], resid_up[None])


class Place:
    def __init__(self, n, send_sems, recv_sems):
        self.m = n.bit_length() - 1
        self.Q = n // 4
        self.me = lax.axis_index("row")
        self.core = lax.axis_index("outer")
        m = self.m
        delta = [(1 - 2 * ((self.me // 2**b) % 2)) * 2**b for b in range(m)]
        self.delta = delta
        self.slot_delta = [delta[m - 1 - i] for i in range(m - 2)] + [delta[0], delta[1]]
        self.near = {"row": self.me + (1 - self.core) * delta[0] + self.core * delta[1]}
        self.far = {"row": self.me + (1 - self.core) * delta[1] + self.core * delta[0]}
        self.peers = [
            {"row": self.me + sum(((p // 2**i) % 2) * delta[m - 1 - i] for i in range(m - 2))}
            for p in range(self.Q)
        ]
        self.twin = {"outer": 1 - self.core}
        self.sems = (send_sems, recv_sems)
        self.sent = []

    def block_of(self, q):
        place = self.me
        for i in range(self.m):
            place = place + ((q // 2**i) % 2) * self.slot_delta[i]
        return place

    def greet(self):
        barrier = pltpu.get_barrier_semaphore()
        targets = self.peers[1:] + [
            {"row": self.me + self.delta[0]}, {"row": self.me + self.delta[1]}, self.twin,
        ]
        for target in targets:
            pl.semaphore_signal(barrier, inc=1, device_id=target, device_id_type=MESH)
        return lambda: pl.semaphore_wait(barrier, len(targets))

    def push(self, src, dst, target):
        i = len(self.sent)
        copy = pltpu.make_async_remote_copy(
            src_ref=src, dst_ref=dst, send_sem=self.sems[0].at[i], recv_sem=self.sems[1].at[i],
            device_id=target, device_id_type=MESH,
        )
        copy.start()
        self.sent.append(copy)
        return copy


class Gather:
    def __init__(self, place, ref):
        self.at = place
        self.ref = ref
        self.moves = {}
        self.swaps = {}

    def go(self, name, src, dst, size, target):
        core = self.at.core
        copy = self.at.push(
            self.ref.at[pl.ds(src, size), core], self.ref.at[pl.ds(dst, size), core], target
        )
        self.moves[name] = (copy, dst, size)

    def start(self):
        for p in range(1, self.at.Q):
            self.go(p, 0, p, 1, self.at.peers[p])

    def spread(self):
        Q, core = self.at.Q, self.at.core
        for p in range(1, Q):
            self.moves[p][0].wait_recv()
        self.go("near", 0, (1 + core) * Q, Q, self.at.near)
        self.go("far", 0, (2 - core) * Q, Q, self.at.far)
        self.swap("peers", 1, Q - 1)

    def pass_on(self):
        Q, core = self.at.Q, self.at.core
        self.moves["near"][0].wait_recv()
        self.go("last", (1 + core) * Q, 3 * Q, Q, self.at.far)
        self.land("near")
        self.land("far")

    def land(self, name):
        copy, dst, size = self.moves[name]
        if name != "near":
            copy.wait_recv()
        self.swap(name, dst, size)

    def swap(self, name, dst, size):
        region = self.ref.at[pl.ds(dst, size), self.at.core]
        self.swaps[name] = self.at.push(region, region, self.at.twin)

    def swapped(self, *names):
        for name in names:
            self.swaps[name].wait_recv()


def forward_kernel(
    n, pods, g0_ref, g1_ref, b0_ref, b1_ref, grads,
    prt_ref, basis, pacc, ptsend, ptrecv, sfull, acc, csend, crecv, rsend, rrecv, gsend, grecv, own,
    send_sems, recv_sems, g_sems, b_sems,
):
    at = Place(n, send_sems, recv_sems)
    upper = project_part(
        at, n, g0_ref, g1_ref, b0_ref, b1_ref, grads, basis, pacc, ptsend, ptrecv, g_sems,
        b_sems,
    )
    copies = [next(upper)]

    def round_product(mat):
        copies[mat].wait_recv()
        prt_ref[mat] = ((ptsend[mat] + ptrecv[mat]) / pods).astype(jnp.bfloat16)
        rows, rank = prt_ref.shape[2], prt_ref.shape[1]
        grads[mat, rows + rank :, :rows] = prt_ref[mat]
        gsend[mat, 0] = contract_cols(prt_ref[mat], prt_ref[mat])

    reduce_part(
        at, n, pods, b0_ref.shape[1], upper, copies, round_product, grads, prt_ref,
        sfull, acc, csend, crecv, rsend, rrecv, gsend, grecv, own,
    )
    for copy in at.sent:
        copy.wait_send()


def pack_of(rank, rows, cols):
    return rows + rank, rows, rows + 3 * cols


def terms(value):
    top = value.astype(jnp.bfloat16)
    rest = value - top.astype(jnp.float32)
    middle = rest.astype(jnp.bfloat16)
    return top, middle, (rest - middle.astype(jnp.float32)).astype(jnp.bfloat16)


def project_part(
    at, n, g0_ref, g1_ref, b0_ref, b1_ref, grads, basis, pacc, ptsend, ptrecv, g_sems,
    b_sems,
):
    m, Q = at.m, at.Q
    rank, cols = b0_ref.shape
    grad_refs = (g0_ref, g1_ref)
    basis_refs = (b0_ref, b1_ref)

    def columns(q):
        return pl.ds(pl.multiple_of(at.block_of(q) * cols, 128), cols)

    def load(mat, q):
        return pltpu.make_async_copy(
            grad_refs[mat].at[0, :, columns(q)], grads.at[mat, pl.ds(0, grad_refs[mat].shape[1]), columns(q)],
            g_sems.at[mat * n + q],
        )

    greeted = at.greet()
    own = [
        pltpu.make_async_copy(
            basis_refs[mat].at[pl.ds(part * (rank // 2), rank // 2)], basis.at[mat, 0, part],
            b_sems.at[2 * mat + part],
        )
        for mat in range(2)
        for part in range(2)
    ]
    for copy in own:
        copy.start()
    for mat in range(2):
        @pl.loop(0, n)
        def _(q):
            load(mat, q).start()

        pacc[mat] = jnp.zeros(pacc.shape[1:], jnp.float32)
    for copy in own:
        copy.wait()
    greeted()

    def project(mat, base, size):
        @pl.loop(0, size)
        def _(k):
            q = base + k
            load(mat, q).wait()
            pacc[mat] += contract_cols(
                grads[mat, pl.ds(0, grad_refs[mat].shape[1]), columns(q)], basis[mat, q].reshape(rank, cols)
            )

    def exchange(mat):
        ptsend[mat] = pacc[mat].T
        return at.push(ptsend.at[mat], ptrecv.at[mat], at.twin)

    gate, up = (Gather(at, basis.at[mat]) for mat in range(2))
    gate.start()
    project(0, 0, 1)
    gate.spread()
    up.start()
    gate.swapped("peers")
    project(0, 1, Q - 1)
    project(1, 0, 1)
    gate.pass_on()
    up.spread()
    gate.swapped("near", "far")
    project(0, Q, 2 * Q)
    gate.land("last")
    up.swapped("peers")
    project(1, 1, Q - 1)
    gate.swapped("last")
    project(0, 3 * Q, Q)
    yield exchange(0)
    up.pass_on()
    yield
    up.land("last")
    up.swapped("near", "far")
    yield
    project(1, Q, 2 * Q)
    up.swapped("last")
    project(1, 3 * Q, Q)
    yield exchange(1)


def reduce_part(
    at, n, pods, cols, upper, copies, round_product, grads, prt_ref,
    sfull, acc, csend, crecv, rsend, rrecv, gsend, grecv, own,
):
    m, Q, core, near, far = at.m, at.Q, at.core, at.near, at.far
    rank, rows = prt_ref.shape[1:]
    half = rank // 2
    row_spot, own_spot, linv_spot = pack_of(rank, rows, cols)

    def columns(q):
        return pl.ds(pl.multiple_of(at.block_of(q) * cols, 128), cols)

    def gram_tasks():
        spot = 0
        for k, targets in enumerate(
            (at.peers[1:], [{"row": at.me + at.delta[1]}], [{"row": at.me + at.delta[0]}])
        ):
            moves = [
                [
                    at.push(gsend.at[mat, k], grecv.at[mat, spot + i], target)
                    for i, target in enumerate(targets)
                ]
                for mat in range(2)
            ]
            yield
            for mat in range(2):
                total = gsend[mat, k]
                for i, move in enumerate(moves[mat]):
                    move.wait_recv()
                    total = total + grecv[mat, spot + i]
                gsend[mat, k + 1] = total
            spot += len(targets)
        sub = lax.broadcasted_iota(jnp.int32, (rank, 2 * rank), 0)
        lane = lax.broadcasted_iota(jnp.int32, (rank, 2 * rank), 1)
        unit = jnp.where(lane == sub + rank, 1.0, 0.0).astype(jnp.float32)[:, rank:]
        systems = [jnp.concatenate([gsend[mat, 3], unit], axis=1) for mat in range(2)]
        for k in range(rank):
            for mat in range(2):
                system = systems[mat]
                scale = 1.0 / jnp.sqrt(system[k : k + 1, k : k + 1])
                row = system[k : k + 1, :] * scale
                column = system[:, k : k + 1] * scale
                systems[mat] = jnp.where(
                    sub == k, row, jnp.where(sub > k, system - column * row, system)
                )
            if k % 8 == 7 and k < rank - 1:
                yield
        for mat in range(2):
            for part, value in enumerate(terms(systems[mat][:, rank:])):
                start = linv_spot + part * 128
                grads[mat, row_spot:, start : start + rank] = value

    core_copy = [{}, {}]
    moved = [{}, {}]

    def multiply(mat, group):
        @pl.loop(group * Q, (group + 1) * Q)
        def _(q):
            product = jnp.dot(
                prt_ref[mat], grads[mat, pl.ds(0, rows), columns(q)], preferred_element_type=jnp.float32
            )
            low, high = product[:half], product[half:]
            acc[mat, q] = jnp.where(core == 0, low, high)
            csend[mat, q] = jnp.where(core == 0, high, low).astype(jnp.bfloat16)

        region = pl.ds(group * Q, Q)
        core_copy[mat][group] = at.push(csend.at[mat, region], crecv.at[mat, region], at.twin)

    def add_core(mat, group):
        core_copy[mat][group].wait_recv()
        region = pl.ds(group * Q, Q)
        acc[mat, region] += crecv[mat, region].astype(jnp.float32)

    def reduce_send(mat, name, base, size, place, target):
        spot = pl.ds(place, size)
        rsend[mat, spot] = acc[mat, pl.ds(base, size)].astype(jnp.bfloat16)
        copy = at.push(rsend.at[mat, spot], rrecv.at[mat, spot], target)
        moved[mat][name] = (copy, place, size)

    def reduce_add(mat, name, base):
        copy, place, size = moved[mat][name]
        copy.wait_recv()
        acc[mat, pl.ds(base, size)] += rrecv[mat, pl.ds(place, size)].astype(jnp.float32)

    def product_tasks(mat):
        multiply(mat, 3)
        yield
        multiply(mat, 2)
        yield
        add_core(mat, 3)
        reduce_send(mat, "second", 3 * Q, Q, Q, far)
        multiply(mat, 1)
        yield
        multiply(mat, 0)
        add_core(mat, 2)
        add_core(mat, 1)
        reduce_send(mat, "first", (2 - core) * Q, Q, 0, far)
        yield

    def reduce_tasks(mat):
        reduce_add(mat, "second", (1 + core) * Q)
        reduce_send(mat, "near", (1 + core) * Q, Q, 2 * Q, near)
        yield
        add_core(mat, 0)
        reduce_add(mat, "first", 0)
        yield
        reduce_add(mat, "near", 0)
        rsend[mat, pl.ds(3 * Q, Q - 1)] = acc[mat, pl.ds(1, Q - 1)].astype(jnp.bfloat16)
        for p in range(1, Q):
            spot = pl.ds(3 * Q + p - 1, 1)
            moved[mat][p] = (
                at.push(rsend.at[mat, spot], rrecv.at[mat, spot], at.peers[p]), 3 * Q + p - 1, 1,
            )
        yield
        for p in range(1, Q):
            reduce_add(mat, p, 0)
        mine = acc[mat, 0] / pods
        own[mat, core] = mine
        sfull[mat, 0, core] = mine.astype(jnp.bfloat16)
        gather = Gather(at, sfull.at[mat])
        gather.start()
        own_copy = at.push(own.at[mat, core], own.at[mat, core], at.twin)
        gather.swap("own", 0, 1)
        yield
        gather.spread()
        yield
        gather.pass_on()
        yield
        gather.land("last")
        yield
        own_copy.wait_recv()
        for part, value in enumerate(terms(own[mat].reshape(rank, cols))):
            start = own_spot + part * cols
            grads[mat, row_spot:, start : start + cols] = value
        gather.swapped(*gather.swaps)

        @pl.loop(0, n)
        def _(q):
            grads[mat, pl.ds(rows, rank), columns(q)] = sfull[mat, q].reshape(rank, cols)

        yield

    def drive(tasks):
        live = list(tasks)
        while live:
            for task in list(live):
                if next(task, StopIteration) is StopIteration:
                    live.remove(task)

    round_product(0)
    gate_product = product_tasks(0)
    next(gate_product)
    next(upper)
    next(gate_product)
    next(gate_product)
    next(upper)
    next(gate_product)
    copies.append(next(upper))
    gate_reduce = reduce_tasks(0)
    next(gate_reduce)
    round_product(1)
    gram = gram_tasks()
    next(gram)
    up_reduce = reduce_tasks(1)
    up_product = product_tasks(1)
    next(up_product)
    next(up_product)
    next(gate_reduce)
    next(up_product)
    next(up_product)
    drive([gate_reduce, up_reduce, gram])


def residual_kernel(
    width, rank, rows, cols, grads,
    next0_ref, next1_ref, factor0_ref, factor1_ref, r0_ref, r1_ref, left, made, sems,
):
    row_spot, own_spot, linv_spot = pack_of(rank, rows, cols)
    tile = 256 if width % 256 == 0 else 128
    steps = grads.shape[2] // width
    for mat, (next_ref, factor_ref) in enumerate(
        ((next0_ref, factor0_ref), (next1_ref, factor1_ref))
    ):
        def whole(start, size, step):
            parts = [
                grads[mat, row_spot:, start + k * step : start + k * step + size].astype(jnp.float32)
                for k in range(3)
            ]
            return parts[0] + (parts[1] + parts[2])

        inverse = whole(linv_spot, rank, 128)
        next_ref[...] = jnp.dot(inverse, whole(own_spot, cols, cols), precision=HIGHEST)
        product = grads[mat, row_spot:, :rows].astype(jnp.float32)
        rows_t = jnp.dot(inverse, product, precision=HIGHEST)
        factor_ref[...] = rows_t
        mixed = lax.dot_general(inverse, rows_t, (((0,), (0,)), ((), ())), precision=HIGHEST).T
        top = mixed.astype(jnp.bfloat16)
        rest = (mixed - top.astype(jnp.float32)).astype(jnp.bfloat16)
        left[mat] = jnp.concatenate([top, rest], axis=1)

    def store(mat, i):
        slot = i % 2
        start = pl.multiple_of(i * width, 128)
        return pltpu.make_async_copy(
            made.at[mat, slot], (r0_ref, r1_ref)[mat].at[0, :, pl.ds(start, width)],
            sems.at[mat, slot],
        )

    @pl.loop(0, steps)
    def _(i):
        for mat in range(2):
            @pl.when(i >= 2)
            def _():
                store(mat, i - 2).wait()

            for k in range(width // tile):
                here = pl.ds(pl.multiple_of(i * width + k * tile, 128), tile)
                block = grads[mat, rows : rows + rank, here]
                product = jnp.dot(
                    left[mat], jnp.concatenate([block, block], axis=0),
                    preferred_element_type=jnp.float32,
                )
                made[mat, i % 2, :, k * tile : (k + 1) * tile] = (
                    grads[mat, :rows, here].astype(jnp.float32) - product
                ).astype(jnp.bfloat16)
            store(mat, i).start()

    for i in range(max(steps - 2, 0), steps):
        for mat in range(2):
            store(mat, i).wait()


def fused(n, pods, grad_gate, grad_up, basis_gate, basis_up):
    _, rows, full_cols = grad_gate.shape
    rank, cols = basis_gate.shape
    half = rank // 2
    vmem = pl.BlockSpec(memory_space=pltpu.VMEM)
    anywhere = pl.BlockSpec(memory_space=pl.ANY)
    hbm = pl.BlockSpec(memory_space=pltpu.HBM)
    f32, bf16 = jnp.float32, jnp.bfloat16
    flops = 4 * rows * full_cols * rank

    def in_hbm(array):
        return pltpu.with_memory_space_constraint(array, pltpu.HBM)

    gather = (n // 4 - 1) + 3 + 4
    count = 2 * (gather + 1 + (n // 4 + 1) + 4 + (n // 4 + 2) + gather + 2)
    packed = pl.pallas_call(
        functools.partial(forward_kernel, n, pods),
        out_shape=pltpu.VMEM((2, rows + 2 * rank, full_cols), bf16),
        in_specs=[anywhere, anywhere, hbm, hbm],
        out_specs=vmem,
        scratch_shapes=[
            pltpu.VMEM((2, rank, rows), bf16),
            pltpu.VMEM((2, n, 2, half, cols), bf16),
            pltpu.VMEM((2, rows, rank), f32),
            pltpu.VMEM((2, rank, rows), f32),
            pltpu.VMEM((2, rank, rows), f32),
            pltpu.VMEM((2, n, 2, half, cols), bf16),
            pltpu.VMEM((2, n, half, cols), f32),
            pltpu.VMEM((2, n, half, cols), bf16),
            pltpu.VMEM((2, n, half, cols), bf16),
            pltpu.VMEM((2, n, half, cols), bf16),
            pltpu.VMEM((2, n, half, cols), bf16),
            pltpu.VMEM((2, 4, rank, rank), f32),
            pltpu.VMEM((2, n // 4 + 1, rank, rank), f32),
            pltpu.VMEM((2, 2, half, cols), f32),
            pltpu.SemaphoreType.DMA((count,)),
            pltpu.SemaphoreType.DMA((count,)),
            pltpu.SemaphoreType.DMA((2 * n,)),
            pltpu.SemaphoreType.DMA((4,)),
        ],
        compiler_params=pltpu.CompilerParams(
            collective_id=0, has_side_effects=True, vmem_limit_bytes=20 * 2**20
        ),
        cost_estimate=pl.CostEstimate(
            flops=2 * flops, bytes_accessed=4 * rows * full_cols, transcendentals=0
        ),
    )(grad_gate, grad_up, in_hbm(basis_gate), in_hbm(basis_up))

    width = next(
        w for w in (1024, 512, 256, 128) if full_cols % w == 0
    )
    next_gate, next_up, factor_gate, factor_up, resid_gate, resid_up = pl.pallas_call(
        functools.partial(residual_kernel, width, rank, rows, cols),
        out_shape=[
            jax.ShapeDtypeStruct((rank, cols), f32),
            jax.ShapeDtypeStruct((rank, cols), f32),
            jax.ShapeDtypeStruct((rank, rows), f32),
            jax.ShapeDtypeStruct((rank, rows), f32),
            jax.ShapeDtypeStruct(grad_gate.shape, bf16),
            jax.ShapeDtypeStruct(grad_up.shape, bf16),
        ],
        in_specs=[vmem],
        out_specs=[vmem] * 4 + [anywhere] * 2,
        scratch_shapes=[
            pltpu.VMEM((2, rows, 2 * rank), bf16),
            pltpu.VMEM((2, 2, rows, width), bf16),
            pltpu.SemaphoreType.DMA((2, 2)),
        ],
        compiler_params=pltpu.CompilerParams(vmem_limit_bytes=20 * 2**20),
        cost_estimate=pl.CostEstimate(
            flops=flops, bytes_accessed=4 * rows * full_cols, transcendentals=0
        ),
    )(packed)
    return next_gate, next_up, factor_gate.T, factor_up.T, resid_gate, resid_up


def dispatch(grad_gate, grad_up, basis_gate, basis_up):
    n = lax.axis_size("row")
    pods = lax.axis_size("outer")
    pod_part, rows, full_cols = grad_gate.shape
    rank, cols = basis_gate.shape
    fits = (
        pods == 2 and pod_part == 1 and n >= 4 and n & (n - 1) == 0
        and cols % 128 == 0 and rows % 128 == 0 and rank % 32 == 0
        and 4 * rows * full_cols <= 32 * 2**20 and rows + 3 * cols + 384 <= full_cols
        and rank <= 128
    )
    if fits:
        return fused(n, pods, grad_gate, grad_up, basis_gate, basis_up)
    return local(grad_gate, grad_up, basis_gate, basis_up)


def solution(mesh):
    return jax.shard_map(
        dispatch,
        mesh=mesh,
        in_specs=(P("outer", "row", None), P("outer", "row", None), P(None, "row"), P(None, "row")),
        out_specs=(
            P(None, "row"),
            P(None, "row"),
            P("row", None),
            P("row", None),
            P("outer", "row", None),
            P("outer", "row", None),
        ),
        check_vma=False,
    )
```
